32 devices in a mesh: dim: 4 (over y, core), rows: 8 (over z, x).
Axes of the slice: x: 2, y: 2, z: 4, core: 2. Of those that a mesh axis runs over, the one named last changes fastest.
Arguments:
- user_rows: bfloat16 [512, 1024], P('rows', 'dim'), may hold values from -0.1875 to 0.1875
- item_table: bfloat16 [8192, 1024], P('rows', 'dim')
- observed_items: int32 [512, 32], P('rows'), may hold values from 0 to 8191, as said below
- counts: int32 [512], P('rows'), may hold values from 1 to 32
- item_row: int32 [8192], replicated, may hold values from 0 to 8191, as said below
Outputs:
- new_users: float32 [512, 1024], P('rows', 'dim')
The draws below stay inside these ranges and needn't reach their ends.
Inputs may be any that keep to these rules, and one draw needn't show every extreme that they name: item_row is a permutation; rows k * 1024 to (k + 1) * 1024 - 1 of item_table form item block k. In the rows of observed_items of each 64 consecutive users (padding slots included), exactly 256 slots name items whose table row lies in item block k, for every k.
All inputs are finite; a program needn't handle non-finite values.
Results may differ from the reference program's by a relative error of at most 0.0003.
Values may be sent and summed in bfloat16 or wider, within the bound.
A program may use at most 64 MiB of HBM per device.

```python
import jax
import jax.numpy as jnp
from jax import lax

BLOCK = 256
LIST = 32
USERS_DEV = 64
ITEM_DEV = 1024
EMBED = 1024
ITEMS = 8192
USERS = 512
N_ROWS = 8


def cluster_count():
    return max(ITEM_DEV // 16, 1)


def shared_layout(key):
    folded = jax.random.fold_in(key, 11)
    perm_key, owner_key, slot_key, taste_key = jax.random.split(folded, 4)
    item_order = jax.random.permutation(perm_key, ITEMS).astype(jnp.int32)
    slots_dev = USERS_DEV * LIST
    per_owner = slots_dev // N_ROWS
    nclusters = cluster_count()
    members = ITEM_DEV // nclusters

    def one_device(device_index):
        owners = jax.random.permutation(jax.random.fold_in(owner_key, device_index), slots_dev).astype(jnp.int32) // per_owner
        tastes = jax.random.randint(jax.random.fold_in(taste_key, device_index), (USERS_DEV, 2), 0, nclusters, dtype=jnp.int32)
        slot_index = jnp.arange(slots_dev, dtype=jnp.int32)
        user_local = slot_index // LIST
        position = slot_index % LIST
        chosen = jnp.where(position % 2 == 0, tastes[user_local, 0], tastes[user_local, 1])
        member = jax.random.randint(jax.random.fold_in(slot_key, device_index), (slots_dev,), 0, members, dtype=jnp.int32)
        within = chosen + nclusters * member
        return owners * ITEM_DEV + within
    table_slots = jax.vmap(one_device)(jnp.arange(N_ROWS, dtype=jnp.int32))
    inverse_order = jnp.argsort(item_order).astype(jnp.int32)
    item_ids = inverse_order[table_slots.reshape(-1)].reshape(USERS, LIST)
    return (item_order, item_ids)


def draw_item_row(key, part):
    return shared_layout(key)[0]


def draw_observed_items(key, part):
    return shared_layout(key)[1]


def draw_item_table(key, part):
    folded = jax.random.fold_in(key, 3)
    noise_key, scale_key, center_key, load_key = jax.random.split(folded, 4)
    nclusters = cluster_count()
    factors = 16
    noise_part = jax.random.normal(noise_key, (ITEMS, EMBED), jnp.float32)
    centers = jax.random.normal(center_key, (factors, nclusters, EMBED), jnp.float32)
    loadings = jax.random.normal(load_key, (ITEMS, factors), jnp.float32)
    item_scale = jnp.exp(jax.random.uniform(scale_key, (ITEMS, 1), jnp.float32, -1.0, 1.0))
    row_cluster = jnp.arange(ITEMS, dtype=jnp.int32) % ITEM_DEV % nclusters
    signal = jnp.zeros((ITEMS, EMBED), jnp.float32)
    for factor_index in range(factors):
        weight_now = 0.6 * 10.0 ** (-1.5 * factor_index / (factors - 1))
        signal = signal + (weight_now * loadings[:, factor_index])[:, None] * centers[factor_index][row_cluster]
    return (item_scale * (signal + 0.3 * noise_part)).astype(jnp.bfloat16)


def touch_ends(drawn, key, smallest, largest):
    spot = [jax.random.randint(jax.random.fold_in(key, axis), (), 0, length) for axis, length in enumerate(drawn.shape)]
    longest = drawn.shape.index(max(drawn.shape))
    next_to = spot[:longest] + [(spot[longest] + 1) % drawn.shape[longest]] + spot[longest + 1:]
    return drawn.at[tuple(spot)].set(smallest).at[tuple(next_to)].set(largest)


def levels(key, shape, shards, smallest, top_value):
    gain = 1.0
    for dim, blocks in shards:
        heights = jax.random.uniform(jax.random.fold_in(jax.random.fold_in(key, 6), dim), (blocks,), jnp.float32, smallest / len(shards), top_value / len(shards))
        gain = gain * jnp.repeat(jnp.exp(heights), shape[dim] // blocks).reshape((-1,) + (1,) * (len(shape) - 1 - dim))
    return gain


def centred(rng, shape, deviation, reach, pieces=(), held_as=jnp.bfloat16):
    drawn = jax.random.normal(rng, shape, jnp.float32) * deviation
    if len(pieces) > 0:
        drawn = levels(rng, shape, pieces, -0.22, 0.18) * drawn
    return jnp.clip(drawn, min=-reach, max=reach).astype(held_as)


def setup_inputs(seed: int = 0) -> dict:
    seeds = jax.random.split(jax.random.key(seed), 6)
    return {
        "user_rows": centred(seeds[0], (USERS, EMBED), EMBED ** -0.5, 0.1875, ((0, 8), (1, 4))),
        "item_table": draw_item_table(jax.random.fold_in(seeds[5], 71), 0),
        "observed_items": draw_observed_items(jax.random.fold_in(seeds[5], 71), 0),
        "counts": touch_ends(jax.random.randint(seeds[3], (USERS,), 1, LIST + 1), jax.random.fold_in(seeds[3], 1), 1, LIST).astype(jnp.int32),
        "item_row": draw_item_row(jax.random.fold_in(seeds[5], 71), 0),
    }


def reference(user_rows, item_table, observed_items, counts, item_row):
    highest = lax.Precision.HIGHEST
    nblocks = EMBED // BLOCK
    weight_unobs = 32.0 / ITEMS
    gram_matrix = jnp.dot(item_table.T.astype(jnp.float32), item_table.astype(jnp.float32), preferred_element_type=jnp.float32)
    gram_times = jnp.dot(user_rows.astype(jnp.float32), gram_matrix, precision=highest)
    diag_blocks = jnp.stack([gram_matrix[n * BLOCK:(n + 1) * BLOCK, n * BLOCK:(n + 1) * BLOCK] for n in range(nblocks)])
    diag_shift = weight_unobs * diag_blocks + jnp.eye(BLOCK, dtype=jnp.float32)
    table_rows = item_row[observed_items]
    live = (lax.broadcasted_iota(jnp.int32, (USERS, LIST), 1) < counts[:, None]).astype(jnp.float32)

    def solve_users(inputs):
        users_here, rows_here, live_here, times_here = inputs
        fetched = item_table[rows_here].astype(jnp.float32)
        predicted = jnp.einsum('ue,uje->uj', users_here.astype(jnp.float32), fetched, precision=highest)
        residual = live_here * (predicted - 1.0)
        fetched_blocks = fetched.reshape(8, LIST, nblocks, BLOCK) * live_here[:, :, None, None]
        hessian = jnp.einsum('ujna,ujnb->unab', fetched_blocks, fetched_blocks, precision=highest) + diag_shift
        own_blocks = users_here.astype(jnp.float32).reshape(8, nblocks, BLOCK)
        gradient = jnp.einsum('uj,ujnb->unb', residual, fetched_blocks, precision=highest)
        gradient = gradient + weight_unobs * times_here.reshape(8, nblocks, BLOCK) + own_blocks
        factor = jnp.linalg.cholesky(hessian)
        middle = jax.scipy.linalg.solve_triangular(factor, gradient[..., None], lower=True)
        update = jax.scipy.linalg.solve_triangular(factor, middle, lower=True, trans='T')[..., 0]
        return (own_blocks - update).reshape(8, EMBED)
    result = lax.map(solve_users, (user_rows.reshape(-1, 8, EMBED), table_rows.reshape(-1, 8, LIST), live.reshape(-1, 8, LIST), gram_times.reshape(-1, 8, EMBED)))
    return result.reshape(USERS, EMBED)
```

```python
import functools

import jax
import jax.numpy as jnp
from jax import lax
from jax.experimental import pallas as pl
from jax.experimental.pallas import tpu as pltpu
from jax.sharding import PartitionSpec as P

F32 = jnp.float32
BF16 = jnp.bfloat16
HIGHEST = lax.Precision.HIGHEST
PANEL = 32


def split3(x):
    high = x.astype(BF16)
    rest = x - high.astype(F32)
    middle = rest.astype(BF16)
    low = (rest - middle.astype(F32)).astype(BF16)
    return high, middle, low


def dot(a, b, dims):
    return lax.dot_general(a, b, (dims, ((), ())), preferred_element_type=F32)


def exact_dot(a, b, dims):
    return lax.dot_general(
        a, b, (dims, ((), ())), precision=HIGHEST, preferred_element_type=F32
    )


def inverse_kernel(weight, gram_ref, out_ref, work):
    width = gram_ref.shape[0]
    rows = lax.broadcasted_iota(jnp.int32, (width, width), 0)
    columns = lax.broadcasted_iota(jnp.int32, (width, width), 1)
    work[...] = weight * gram_ref[...] + jnp.where(rows == columns, 1.0, 0.0)
    panel_rows = lax.broadcasted_iota(jnp.int32, (PANEL, 1), 0)
    panel_columns = lax.broadcasted_iota(jnp.int32, (PANEL, width), 1)
    for panel in range(width // PANEL):
        first = panel * PANEL
        mine = (panel_columns >= first) & (panel_columns < first + PANEL)
        before = work[first:first + PANEL, :]
        after = before
        for step in range(PANEL):
            column = after[:, first + step:first + step + 1]
            inverse = 1.0 / column[step:step + 1, :]
            unit = jnp.where(panel_rows == step, 1.0, 0.0)
            after = jnp.where(panel_columns == first + step, unit, after)
            scaled = after[step:step + 1, :] * inverse
            after = jnp.where(panel_rows == step, scaled, after - column * scaled)
        after = jnp.where(mine, -after, after)
        sign = jnp.where(panel_columns == first + lax.broadcasted_iota(jnp.int32, (PANEL, width), 0), -1.0, 0.0)
        before = jnp.where(mine, sign, before)
        b1, b2, b3 = split3(before)
        a1, a2, a3 = split3(after)
        left = jnp.concatenate([b1, b1, b2, b1, b2, b3], axis=0)
        right = jnp.concatenate([a1, a2, a1, a3, a2, a1], axis=0)
        change = dot(left, right, ((0,), (0,)))
        outside = ((rows < first) | (rows >= first + PANEL)) & (
            (columns < first) | (columns >= first + PANEL)
        )
        work[...] = jnp.where(outside, work[...], 0.0) - change
    out_ref[...] = -work[...]


def own_slots(users, list_len):
    row = lax.broadcasted_iota(jnp.int32, (users, users * list_len), 0)
    column = lax.broadcasted_iota(jnp.int32, (users, users * list_len), 1)
    return (column >= row * list_len) & (column < (row + 1) * list_len)


def fold_lanes(x, list_len):
    lanes = 128
    total = x[:, :lanes]
    for part in range(1, x.shape[1] // lanes):
        total = total + x[:, part * lanes:(part + 1) * lanes]
    result = total[:, :list_len]
    for part in range(1, lanes // list_len):
        result = result + total[:, part * list_len:(part + 1) * list_len]
    return result


def spread_lanes(x, users):
    lanes = 128
    tile = jnp.concatenate([x] * (lanes // x.shape[1]), axis=1)
    return jnp.concatenate([tile] * (users * x.shape[1] // lanes), axis=1)


def solve_kernel(
    weight, rows_ref, live_ref, predicted_ref, inverse_ref, times_ref, own_ref, out_ref,
    scaled, folded, system,
):
    users, list_len = live_ref.shape
    own = own_ref[...].astype(F32)
    h = rows_ref[...]
    mask = own_slots(users, list_len)
    residual = live_ref[...] * (predicted_ref[...] - 1.0)
    spread = jnp.where(mask, spread_lanes(residual, users), 0.0)
    gradient = weight * times_ref[...] + own
    for piece in split3(spread):
        gradient = gradient + dot(piece, h, ((1,), (0,)))
    inverse = inverse_ref[...]
    scaled_grad = exact_dot(gradient, inverse, ((1,), (0,)))
    projected = jnp.zeros((users, users * list_len), F32)
    for piece in split3(scaled_grad):
        projected = projected + dot(piece, h, ((1,), (1,)))
    projected = fold_lanes(jnp.where(mask, projected, 0.0), list_len).T

    inverse_pieces = split3(inverse)
    group = 8 * list_len
    block_row = lax.broadcasted_iota(jnp.int32, (group, group), 0) // list_len
    block_column = lax.broadcasted_iota(jnp.int32, (group, group), 1) // list_len
    for start in range(0, users * list_len, group):
        here = rows_ref[start:start + group, :]
        x = sum(dot(here, piece, ((1,), (0,))) for piece in inverse_pieces)
        inner = sum(dot(piece, here, ((1,), (1,))) for piece in split3(x))
        inner = jnp.where(block_row == block_column, inner, 0.0)
        folded[start:start + group, :] = fold_lanes(inner, list_len)
    slot = lax.broadcasted_iota(jnp.int32, (list_len, users), 0)
    head = lax.broadcasted_iota(jnp.int32, (8, users), 0)
    for i in range(list_len):
        block = folded[pl.ds(i, users, stride=list_len), :].T
        system[i, :list_len, :] = block + jnp.where(slot == i, 1.0, 0.0)
        system[i, list_len:, :] = jnp.where(head == 0, projected[i:i + 1, :], 0.0)
    for k in range(list_len):
        first = k // 8 * 8
        pivot_row = system[k, first:, :]
        pivot_row = pivot_row * (1.0 / system[k, k:k + 1, :])
        for i in range(list_len):
            if i != k:
                system[i, first:, :] = system[i, first:, :] - system[i, k:k + 1, :] * pivot_row
    weights = jnp.concatenate(
        [system[i, list_len:list_len + 1, :] / system[i, i:i + 1, :] for i in range(list_len)], axis=0
    ).T
    spread = jnp.where(mask, spread_lanes(weights, users), 0.0)
    for piece in split3(spread):
        gradient = gradient - dot(piece, h, ((1,), (0,)))
    out_ref[...] = own - exact_dot(gradient, inverse, ((1,), (0,)))


def on_device(user_rows, item_table, observed_items, counts, item_row):
    width = user_rows.shape[1]
    users_dev, list_len = observed_items.shape
    weight_unobs = 32.0 / item_row.shape[0]
    vmem = pl.BlockSpec(memory_space=pltpu.VMEM)

    shard_rows = lax.all_gather(item_table, "rows", axis=0, tiled=True)
    full_rows = lax.all_gather(item_table, "dim", axis=1, tiled=True)
    all_users = lax.all_gather(lax.all_gather(user_rows, "dim", axis=1, tiled=True), "rows", axis=0, tiled=True)
    scores = dot(all_users, full_rows, ((1,), (1,)))
    times_part = exact_dot(scores, item_table.astype(F32), ((1,), (0,)))
    gram_times = lax.psum_scatter(times_part, "rows", scatter_dimension=0, tiled=True)
    diag_gram = dot(shard_rows, shard_rows, ((0,), (0,)))

    table_rows = item_row[observed_items]
    live = lax.broadcasted_iota(jnp.int32, (users_dev, list_len), 1) < counts[:, None]
    picked = shard_rows[table_rows]
    fetched = jnp.where(live[..., None], picked, jnp.zeros_like(picked))
    predicted = lax.psum(
        jnp.einsum("ub,ujb->uj", user_rows, fetched, preferred_element_type=F32), "dim"
    )

    inverse = pl.pallas_call(
        functools.partial(inverse_kernel, weight_unobs),
        out_shape=jax.ShapeDtypeStruct((width, width), F32),
        in_specs=[vmem],
        out_specs=vmem,
        scratch_shapes=[pltpu.VMEM((width, width), F32)],
        name="inverse",
    )(diag_gram)
    return pl.pallas_call(
        functools.partial(solve_kernel, weight_unobs),
        out_shape=jax.ShapeDtypeStruct((users_dev, width), F32),
        in_specs=[vmem] * 6,
        out_specs=vmem,
        scratch_shapes=[
            pltpu.VMEM((8, 128), F32),
            pltpu.VMEM((users_dev * list_len, list_len), F32),
            pltpu.VMEM((list_len, list_len + 8, users_dev), F32),
        ],
        compiler_params=pltpu.CompilerParams(vmem_limit_bytes=48 * 1024 * 1024),
        name="solve",
    )(
        fetched.reshape(users_dev * list_len, width), live.astype(F32), predicted, inverse,
        gram_times, user_rows,
    )


def solution(mesh):
    in_specs = (P("rows", "dim"), P("rows", "dim"), P("rows", None), P("rows"), P())
    out_specs = P("rows", "dim")
    return jax.shard_map(
        on_device, mesh=mesh, in_specs=in_specs, out_specs=out_specs, check_vma=False
    )
```

```python
import functools

import jax
import jax.numpy as jnp
from jax import lax
from jax.experimental import pallas as pl
from jax.experimental.pallas import tpu as pltpu
from jax.sharding import PartitionSpec as P

F32 = jnp.float32
BF16 = jnp.bfloat16
HIGHEST = lax.Precision.HIGHEST
PANEL = 32


def split3(x):
    high = x.astype(BF16)
    rest = x - high.astype(F32)
    middle = rest.astype(BF16)
    low = (rest - middle.astype(F32)).astype(BF16)
    return high, middle, low


def dot(a, b, dims):
    return lax.dot_general(a, b, (dims, ((), ())), preferred_element_type=F32)


def exact_dot(a, b, dims):
    return lax.dot_general(
        a, b, (dims, ((), ())), precision=HIGHEST, preferred_element_type=F32
    )


def inverse_kernel(weight, gram_ref, out_ref, work):
    width = gram_ref.shape[0]
    rows = lax.broadcasted_iota(jnp.int32, (width, width), 0)
    columns = lax.broadcasted_iota(jnp.int32, (width, width), 1)
    work[...] = weight * gram_ref[...] + jnp.where(rows == columns, 1.0, 0.0)
    panel_rows = lax.broadcasted_iota(jnp.int32, (PANEL, 1), 0)
    panel_columns = lax.broadcasted_iota(jnp.int32, (PANEL, width), 1)
    for panel in range(width // PANEL):
        first = panel * PANEL
        mine = (panel_columns >= first) & (panel_columns < first + PANEL)
        before = work[first:first + PANEL, :]
        after = before
        for step in range(PANEL):
            column = after[:, first + step:first + step + 1]
            inverse = 1.0 / column[step:step + 1, :]
            unit = jnp.where(panel_rows == step, 1.0, 0.0)
            after = jnp.where(panel_columns == first + step, unit, after)
            scaled = after[step:step + 1, :] * inverse
            after = jnp.where(panel_rows == step, scaled, after - column * scaled)
        after = jnp.where(mine, -after, after)
        sign = jnp.where(panel_columns == first + lax.broadcasted_iota(jnp.int32, (PANEL, width), 0), -1.0, 0.0)
        before = jnp.where(mine, sign, before)
        b1, b2, b3 = split3(before)
        a1, a2, a3 = split3(after)
        left = jnp.concatenate([b1, b1, b2, b1, b2, b3], axis=0)
        right = jnp.concatenate([a1, a2, a1, a3, a2, a1], axis=0)
        change = dot(left, right, ((0,), (0,)))
        outside = ((rows < first) | (rows >= first + PANEL)) & (
            (columns < first) | (columns >= first + PANEL)
        )
        work[...] = jnp.where(outside, work[...], 0.0) - change
    out_ref[...] = -work[...]


def own_slots(users, list_len):
    row = lax.broadcasted_iota(jnp.int32, (users, users * list_len), 0)
    column = lax.broadcasted_iota(jnp.int32, (users, users * list_len), 1)
    return (column >= row * list_len) & (column < (row + 1) * list_len)


def fold_lanes(x, list_len):
    lanes = 128
    total = x[:, :lanes]
    for part in range(1, x.shape[1] // lanes):
        total = total + x[:, part * lanes:(part + 1) * lanes]
    result = total[:, :list_len]
    for part in range(1, lanes // list_len):
        result = result + total[:, part * list_len:(part + 1) * list_len]
    return result


def spread_lanes(x, users):
    lanes = 128
    tile = jnp.concatenate([x] * (lanes // x.shape[1]), axis=1)
    return jnp.concatenate([tile] * (users * x.shape[1] // lanes), axis=1)


def solve_kernel(
    weight, rows_ref, live_ref, predicted_ref, inverse_ref, times_ref, own_ref, out_ref,
    scaled, folded, system,
):
    users, list_len = live_ref.shape
    own = own_ref[...].astype(F32)
    h = rows_ref[...]
    mask = own_slots(users, list_len)
    residual = live_ref[...] * (predicted_ref[...] - 1.0)
    spread = jnp.where(mask, spread_lanes(residual, users), 0.0)
    gradient = weight * times_ref[...] + own
    for piece in split3(spread):
        gradient = gradient + dot(piece, h, ((1,), (0,)))
    inverse = inverse_ref[...]
    scaled_grad = exact_dot(gradient, inverse, ((1,), (0,)))
    projected = jnp.zeros((users, users * list_len), F32)
    for piece in split3(scaled_grad):
        projected = projected + dot(piece, h, ((1,), (1,)))
    projected = fold_lanes(jnp.where(mask, projected, 0.0), list_len).T

    inverse_pieces = split3(inverse)
    group = 8 * list_len
    block_row = lax.broadcasted_iota(jnp.int32, (group, group), 0) // list_len
    block_column = lax.broadcasted_iota(jnp.int32, (group, group), 1) // list_len
    for start in range(0, users * list_len, group):
        here = rows_ref[start:start + group, :]
        x = sum(dot(here, piece, ((1,), (0,))) for piece in inverse_pieces)
        inner = sum(dot(piece, here, ((1,), (1,))) for piece in split3(x))
        inner = jnp.where(block_row == block_column, inner, 0.0)
        folded[start:start + group, :] = fold_lanes(inner, list_len)
    slot = lax.broadcasted_iota(jnp.int32, (list_len, users), 0)
    head = lax.broadcasted_iota(jnp.int32, (8, users), 0)
    for i in range(list_len):
        block = folded[pl.ds(i, users, stride=list_len), :].T
        system[i, :list_len, :] = block + jnp.where(slot == i, 1.0, 0.0)
        system[i, list_len:, :] = jnp.where(head == 0, projected[i:i + 1, :], 0.0)
    for k in range(list_len):
        first = k // 8 * 8
        pivot_row = system[k, first:, :]
        pivot_row = pivot_row * (1.0 / system[k, k:k + 1, :])
        for i in range(list_len):
            if i != k:
                system[i, first:, :] = system[i, first:, :] - system[i, k:k + 1, :] * pivot_row
    weights = jnp.concatenate(
        [system[i, list_len:list_len + 1, :] / system[i, i:i + 1, :] for i in range(list_len)], axis=0
    ).T
    spread = jnp.where(mask, spread_lanes(weights, users), 0.0)
    for piece in split3(spread):
        gradient = gradient - dot(piece, h, ((1,), (0,)))
    out_ref[...] = own - exact_dot(gradient, inverse, ((1,), (0,)))


MESH = pl.DeviceIdType.MESH


def ring_place(index, n):
    odd = lax.rem(index, 2)
    return (1 - odd) * lax.div(index, 2) + odd * (n // 2 + lax.div(n - 1 - index, 2))


def ring_index(place, n):
    high = lax.div(place, n // 2)
    return (1 - high) * 2 * place + high * (n - 1 - 2 * (place - n // 2))


def exchange_kernel(
    n_rows, n_dim, table_ref, users_ref, gathered_ref, gram_ref, times_ref,
    held, tables, users, staged, arrived,
    ring_send, ring_recv, out_sem, first_send, first_recv, table_send, table_recv,
    users_send, users_recv, sum_send, sum_recv,
):
    me_row = lax.axis_index("rows")
    me_dim = lax.axis_index("dim")
    items, width = table_ref.shape
    users_dev = users_ref.shape[0]
    half = n_rows // 2
    levels = n_dim // 2
    core = lax.rem(me_dim, 2)
    partner = me_dim + 1 - 2 * core
    place = ring_place(me_row, n_rows)
    right = ring_index(lax.rem(place + 1, n_rows), n_rows)
    left = ring_index(lax.rem(place + n_rows - 1, n_rows), n_rows)

    def row_peer(k):
        return lax.rem(me_row + k, n_rows)

    def dim_peer(k):
        return lax.rem(me_dim + 2 * k, n_dim)

    def dim_source(k):
        return lax.rem(me_dim + n_dim - 2 * k, n_dim)

    barrier = pltpu.get_barrier_semaphore()
    for k in range(1, n_rows):
        pl.semaphore_signal(barrier, inc=1, device_id={"rows": row_peer(k)}, device_id_type=MESH)
    for k in range(1, levels):
        pl.semaphore_signal(barrier, inc=1, device_id={"dim": dim_peer(k)}, device_id_type=MESH)
    pl.semaphore_signal(barrier, inc=1, device_id={"dim": partner}, device_id_type=MESH)
    pl.semaphore_wait(barrier, n_rows - 1 + levels)

    def remote(src, dst, send, recv, device):
        copy = pltpu.make_async_remote_copy(
            src_ref=src, dst_ref=dst, send_sem=send, recv_sem=recv,
            device_id=device, device_id_type=MESH,
        )
        copy.start()
        return copy

    def block_of(index, start, size):
        return held.at[pl.ds(index * items + start, size)]

    def ring_step(step):
        copies = []
        last = step == half - 1
        for way, to in ((0, right), (1, left)):
            shift = n_rows - step if way == 0 else step
            owner = ring_index(lax.rem(place + shift, n_rows), n_rows)
            size = items // 2 if last else items
            start = items // 2 if last and way == 1 else 0
            target = block_of(owner, start, size)
            copies.append(remote(
                table_ref.at[pl.ds(start, size)] if step == 0 else target,
                target, ring_send.at[way, step], ring_recv.at[way, step], {"rows": to},
            ))
        return copies

    outs = []

    def keep(index, start, size):
        copy = pltpu.make_async_copy(
            block_of(index, start, size),
            gathered_ref.at[pl.ds(index * items + start, size)],
            out_sem.at[len(outs)],
        )
        copy.start()
        outs.append(copy)

    def add_gram(index, start, size):
        block = held[pl.ds(index * items + start, size), :]
        gram_ref[...] += dot(block, block, ((0,), (0,)))

    def ring_arrivals(step):
        last = step == half - 1
        found = []
        for way in (0, 1):
            shift = n_rows - step - 1 if way == 0 else step + 1
            owner = ring_index(lax.rem(place + shift, n_rows), n_rows)
            size = items // 2 if last else items
            start = items // 2 if last and way == 1 else 0
            found.append((owner, start, size))
        return found

    mine_users = pl.ds(me_row * users_dev, users_dev)
    first = [
        remote(users_ref, users.at[me_dim, mine_users], first_send.at[k], first_recv.at[k], {"rows": row_peer(k)})
        for k in range(1, n_rows)
    ]
    ring = [ring_step(0)]
    table_far = [
        remote(table_ref, tables.at[me_dim], table_send.at[k], table_recv.at[k], {"dim": dim_peer(k)})
        for k in range(1, levels)
    ]
    table_near = [remote(table_ref, tables.at[me_dim], table_send.at[0], table_recv.at[0], {"dim": partner})]
    held[pl.ds(me_row * items, items), :] = table_ref[...]
    tables[me_dim] = table_ref[...]
    users[me_dim, mine_users, :] = users_ref[...]
    gram_ref[...] = jnp.zeros_like(gram_ref)
    keep(me_row, 0, items)
    add_gram(me_row, 0, items)

    for copy in first:
        copy.wait_recv()
    users_far = [
        remote(users.at[me_dim], users.at[me_dim], users_send.at[k], users_recv.at[k], {"dim": dim_peer(k)})
        for k in range(1, levels)
    ]
    users_near = [remote(users.at[me_dim], users.at[me_dim], users_send.at[0], users_recv.at[0], {"dim": partner})]
    sums = []

    def relay():
        for k in range(1, levels):
            source = dim_source(k)
            table_far[k - 1].wait_recv()
            table_near.append(remote(
                tables.at[source], tables.at[source], table_send.at[levels + k], table_recv.at[levels + k], {"dim": partner},
            ))
            users_far[k - 1].wait_recv()
            users_near.append(remote(
                users.at[source], users.at[source], users_send.at[levels + k], users_recv.at[levels + k], {"dim": partner},
            ))

    def score():
        for copy in table_near + users_near:
            copy.wait_recv()
        total = n_rows * users_dev
        chunk = min(256, total)
        pieces_of_table = table_ref[...]
        for start in range(0, total, chunk):
            scores = dot(users[0, start:start + chunk, :], tables[0], ((1,), (1,)))
            for d in range(1, n_dim):
                scores = scores + dot(users[d, start:start + chunk, :], tables[d], ((1,), (1,)))
            part = sum(dot(piece, pieces_of_table, ((1,), (0,))) for piece in split3(scores))
            staged[start:start + chunk, :] = part
        for k in range(1, n_rows):
            sums.append(remote(
                staged.at[pl.ds(row_peer(k) * users_dev, users_dev)], arrived.at[k],
                sum_send.at[k], sum_recv.at[k], {"rows": row_peer(k)},
            ))

    for step in range(half):
        for copy in ring[step]:
            copy.wait_recv()
        if step < half - 1:
            ring.append(ring_step(step + 1))
        for found in ring_arrivals(step):
            keep(*found)
            add_gram(*found)
        if step == 0:
            relay()
        if step == 1:
            score()

    times = staged[mine_users, :]
    for k in range(1, n_rows):
        sums[k - 1].wait_recv()
        times = times + arrived[k]
    times_ref[...] = times
    for copy in first + table_far + table_near + users_far + users_near + sums + ring[0]:
        copy.wait_send()
    for copies in ring[1:]:
        for copy in copies:
            copy.wait_send()
    for copy in outs:
        copy.wait()


def exchange(item_table, user_rows, n_rows, n_dim):
    items, width = item_table.shape
    users_dev = user_rows.shape[0]
    vmem = pl.BlockSpec(memory_space=pltpu.VMEM)
    dma = pltpu.SemaphoreType.DMA
    half = n_rows // 2
    return pl.pallas_call(
        functools.partial(exchange_kernel, n_rows, n_dim),
        out_shape=[
            jax.ShapeDtypeStruct((n_rows * items, width), BF16),
            jax.ShapeDtypeStruct((width, width), F32),
            jax.ShapeDtypeStruct((users_dev, width), F32),
        ],
        in_specs=[vmem] * 2,
        out_specs=[pl.BlockSpec(memory_space=pl.ANY), vmem, vmem],
        scratch_shapes=[
            pltpu.VMEM((n_rows * items, width), BF16),
            pltpu.VMEM((n_dim, items, width), BF16),
            pltpu.VMEM((n_dim, n_rows * users_dev, width), BF16),
            pltpu.VMEM((n_rows * users_dev, width), F32),
            pltpu.VMEM((n_rows, users_dev, width), F32),
            dma((2, half)),
            dma((2, half)),
            dma((n_rows + 1,)),
            dma((n_rows,)),
            dma((n_rows,)),
            dma((n_dim,)),
            dma((n_dim,)),
            dma((n_dim,)),
            dma((n_dim,)),
            dma((n_rows,)),
            dma((n_rows,)),
        ],
        compiler_params=pltpu.CompilerParams(
            collective_id=0, has_side_effects=True, vmem_limit_bytes=56 * 1024 * 1024
        ),
        name="exchange",
    )(item_table, user_rows)


def on_device(user_rows, item_table, observed_items, counts, item_row):
    width = user_rows.shape[1]
    users_dev, list_len = observed_items.shape
    weight_unobs = 32.0 / item_row.shape[0]
    vmem = pl.BlockSpec(memory_space=pltpu.VMEM)

    shard_rows, diag_gram, gram_times = exchange(
        item_table, user_rows, lax.axis_size("rows"), lax.axis_size("dim")
    )

    slots = observed_items.reshape(-1, 1)
    lines = item_row.reshape(-1, 128).astype(F32)
    line_of = lax.broadcasted_iota(jnp.int32, (1, lines.shape[0]), 1) == slots // 128
    chosen = exact_dot(line_of.astype(F32), lines, ((1,), (0,)))
    lane_of = lax.broadcasted_iota(jnp.int32, (1, 128), 1) == slots % 128
    table_rows = jnp.sum(jnp.where(lane_of, chosen, 0.0), axis=1).astype(jnp.int32)
    table_rows = table_rows.reshape(observed_items.shape)
    live = lax.broadcasted_iota(jnp.int32, (users_dev, list_len), 1) < counts[:, None]
    picked = shard_rows[table_rows]
    fetched = jnp.where(live[..., None], picked, jnp.zeros_like(picked))
    predicted = lax.psum(
        jnp.einsum("ub,ujb->uj", user_rows, fetched, preferred_element_type=F32), "dim"
    )

    inverse = pl.pallas_call(
        functools.partial(inverse_kernel, weight_unobs),
        out_shape=jax.ShapeDtypeStruct((width, width), F32),
        in_specs=[vmem],
        out_specs=vmem,
        scratch_shapes=[pltpu.VMEM((width, width), F32)],
        name="inverse",
    )(diag_gram)
    return pl.pallas_call(
        functools.partial(solve_kernel, weight_unobs),
        out_shape=jax.ShapeDtypeStruct((users_dev, width), F32),
        in_specs=[vmem] * 6,
        out_specs=vmem,
        scratch_shapes=[
            pltpu.VMEM((8, 128), F32),
            pltpu.VMEM((users_dev * list_len, list_len), F32),
            pltpu.VMEM((list_len, list_len + 8, users_dev), F32),
        ],
        compiler_params=pltpu.CompilerParams(vmem_limit_bytes=48 * 1024 * 1024),
        name="solve",
    )(
        fetched.reshape(users_dev * list_len, width), live.astype(F32), predicted, inverse,
        gram_times, user_rows,
    )


def solution(mesh):
    in_specs = (P("rows", "dim"), P("rows", "dim"), P("rows", None), P("rows"), P())
    out_specs = P("rows", "dim")
    return jax.shard_map(
        on_device, mesh=mesh, in_specs=in_specs, out_specs=out_specs, check_vma=False
    )
```

```python
import functools

import jax
import jax.numpy as jnp
from jax import lax
from jax.experimental import pallas as pl
from jax.experimental.pallas import tpu as pltpu
from jax.sharding import PartitionSpec as P

F32 = jnp.float32
BF16 = jnp.bfloat16
HIGHEST = lax.Precision.HIGHEST
PANEL = 32
GROUP = 8


def split3(x):
    high = x.astype(BF16)
    rest = x - high.astype(F32)
    middle = rest.astype(BF16)
    low = (rest - middle.astype(F32)).astype(BF16)
    return high, middle, low


def dot(a, b, dims):
    return lax.dot_general(a, b, (dims, ((), ())), preferred_element_type=F32)


def exact_dot(a, b, dims):
    return lax.dot_general(
        a, b, (dims, ((), ())), precision=HIGHEST, preferred_element_type=F32
    )


def inverse_kernel(weight, gram_ref, out_ref, work):
    width = gram_ref.shape[0]
    rows = lax.broadcasted_iota(jnp.int32, (width, width), 0)
    columns = lax.broadcasted_iota(jnp.int32, (width, width), 1)
    work[...] = weight * gram_ref[...] + jnp.where(rows == columns, 1.0, 0.0)
    panel_rows = lax.broadcasted_iota(jnp.int32, (PANEL, 1), 0)
    panel_columns = lax.broadcasted_iota(jnp.int32, (PANEL, width), 1)
    for panel in range(width // PANEL):
        first = panel * PANEL
        mine = (panel_columns >= first) & (panel_columns < first + PANEL)
        before = work[first:first + PANEL, :]
        after = before
        for group in range(0, PANEL, GROUP):
            spread = [
                jnp.broadcast_to(after[:, c:c + 1], (PANEL, 128))
                for c in range(first + group, first + group + GROUP)
            ]
            for step in range(group, group + GROUP):
                column = spread[step - group]
                inverse = 1.0 / column[step:step + 1, :]
                for later in range(step - group + 1, GROUP):
                    other = spread[later]
                    scaled = other[step:step + 1, :] * inverse
                    spread[later] = jnp.where(panel_rows == step, scaled, other - column * scaled)
                wide = jnp.concatenate([column] * (width // 128), axis=1)
                wide_inverse = jnp.concatenate([inverse] * (width // 128), axis=1)
                unit = jnp.where(panel_rows == step, 1.0, 0.0)
                after = jnp.where(panel_columns == first + step, unit, after)
                scaled = after[step:step + 1, :] * wide_inverse
                after = jnp.where(panel_rows == step, scaled, after - wide * scaled)
        after = jnp.where(mine, -after, after)
        sign = jnp.where(panel_columns == first + lax.broadcasted_iota(jnp.int32, (PANEL, width), 0), -1.0, 0.0)
        before = jnp.where(mine, sign, before)
        b1, b2, b3 = split3(before)
        a1, a2, a3 = split3(after)
        left = jnp.concatenate([b1, b1, b2, b1, b2, b3], axis=0)
        right = jnp.concatenate([a1, a2, a1, a3, a2, a1], axis=0)
        change = dot(left, right, ((0,), (0,)))
        outside = ((rows < first) | (rows >= first + PANEL)) & (
            (columns < first) | (columns >= first + PANEL)
        )
        work[...] = jnp.where(outside, work[...], 0.0) - change
    out_ref[...] = -work[...]


def own_slots(users, list_len):
    row = lax.broadcasted_iota(jnp.int32, (users, users * list_len), 0)
    column = lax.broadcasted_iota(jnp.int32, (users, users * list_len), 1)
    return (column >= row * list_len) & (column < (row + 1) * list_len)


def fold_lanes(x, list_len):
    lanes = 128
    total = x[:, :lanes]
    for part in range(1, x.shape[1] // lanes):
        total = total + x[:, part * lanes:(part + 1) * lanes]
    result = total[:, :list_len]
    for part in range(1, lanes // list_len):
        result = result + total[:, part * list_len:(part + 1) * list_len]
    return result


def spread_lanes(x, users):
    lanes = 128
    tile = jnp.concatenate([x] * (lanes // x.shape[1]), axis=1)
    return jnp.concatenate([tile] * (users * x.shape[1] // lanes), axis=1)


def solve_kernel(
    weight, rows_ref, live_ref, predicted_ref, inverse_ref, times_ref, own_ref, out_ref,
    scaled, folded, system,
):
    users, list_len = live_ref.shape
    own = own_ref[...].astype(F32)
    h = rows_ref[...]
    mask = own_slots(users, list_len)
    residual = live_ref[...] * (predicted_ref[...] - 1.0)
    spread = jnp.where(mask, spread_lanes(residual, users), 0.0)
    gradient = weight * times_ref[...] + own
    for piece in split3(spread):
        gradient = gradient + dot(piece, h, ((1,), (0,)))
    inverse = inverse_ref[...]
    scaled_grad = exact_dot(gradient, inverse, ((1,), (0,)))
    projected = jnp.zeros((users, users * list_len), F32)
    for piece in split3(scaled_grad):
        projected = projected + dot(piece, h, ((1,), (1,)))
    projected = fold_lanes(jnp.where(mask, projected, 0.0), list_len).T

    inverse_pieces = split3(inverse)
    group = 8 * list_len
    block_row = lax.broadcasted_iota(jnp.int32, (group, group), 0) // list_len
    block_column = lax.broadcasted_iota(jnp.int32, (group, group), 1) // list_len
    for start in range(0, users * list_len, group):
        here = rows_ref[start:start + group, :]
        x = sum(dot(here, piece, ((1,), (0,))) for piece in inverse_pieces)
        inner = sum(dot(piece, here, ((1,), (1,))) for piece in split3(x))
        inner = jnp.where(block_row == block_column, inner, 0.0)
        folded[start:start + group, :] = fold_lanes(inner, list_len)
    slot = lax.broadcasted_iota(jnp.int32, (list_len, users), 0)
    head = lax.broadcasted_iota(jnp.int32, (8, users), 0)
    for i in range(list_len):
        block = folded[pl.ds(i, users, stride=list_len), :].T
        system[i, :list_len, :] = block + jnp.where(slot == i, 1.0, 0.0)
        system[i, list_len:, :] = jnp.where(head == 0, projected[i:i + 1, :], 0.0)
    for k in range(list_len):
        first = k // 8 * 8
        pivot_row = system[k, first:, :]
        pivot_row = pivot_row * (1.0 / system[k, k:k + 1, :])
        for i in range(list_len):
            if i != k:
                system[i, first:, :] = system[i, first:, :] - system[i, k:k + 1, :] * pivot_row
    weights = jnp.concatenate(
        [system[i, list_len:list_len + 1, :] / system[i, i:i + 1, :] for i in range(list_len)], axis=0
    ).T
    spread = jnp.where(mask, spread_lanes(weights, users), 0.0)
    for piece in split3(spread):
        gradient = gradient - dot(piece, h, ((1,), (0,)))
    out_ref[...] = own - exact_dot(gradient, inverse, ((1,), (0,)))


MESH = pl.DeviceIdType.MESH


def ring_place(index, n):
    odd = lax.rem(index, 2)
    return (1 - odd) * lax.div(index, 2) + odd * (n // 2 + lax.div(n - 1 - index, 2))


def ring_index(place, n):
    high = lax.div(place, n // 2)
    return (1 - high) * 2 * place + high * (n - 1 - 2 * (place - n // 2))


def exchange_kernel(
    n_rows, n_dim, table_ref, users_ref, gathered_ref, gram_ref, times_ref,
    held, tables, users, staged, arrived,
    ring_send, ring_recv, out_sem, first_send, first_recv, table_send, table_recv,
    users_send, users_recv, sum_send, sum_recv,
):
    me_row = lax.axis_index("rows")
    me_dim = lax.axis_index("dim")
    items, width = table_ref.shape
    users_dev = users_ref.shape[0]
    half = n_rows // 2
    levels = n_dim // 2
    core = lax.rem(me_dim, 2)
    partner = me_dim + 1 - 2 * core
    place = ring_place(me_row, n_rows)
    right = ring_index(lax.rem(place + 1, n_rows), n_rows)
    left = ring_index(lax.rem(place + n_rows - 1, n_rows), n_rows)

    def row_peer(k):
        return lax.rem(me_row + k, n_rows)

    def dim_peer(k):
        return lax.rem(me_dim + 2 * k, n_dim)

    def dim_source(k):
        return lax.rem(me_dim + n_dim - 2 * k, n_dim)

    barrier = pltpu.get_barrier_semaphore()
    for k in range(1, n_rows):
        pl.semaphore_signal(barrier, inc=1, device_id={"rows": row_peer(k)}, device_id_type=MESH)
    for k in range(1, levels):
        pl.semaphore_signal(barrier, inc=1, device_id={"dim": dim_peer(k)}, device_id_type=MESH)
    pl.semaphore_signal(barrier, inc=1, device_id={"dim": partner}, device_id_type=MESH)
    pl.semaphore_wait(barrier, n_rows - 1 + levels)

    def remote(src, dst, send, recv, device):
        copy = pltpu.make_async_remote_copy(
            src_ref=src, dst_ref=dst, send_sem=send, recv_sem=recv,
            device_id=device, device_id_type=MESH,
        )
        copy.start()
        return copy

    def block_of(index, start, size):
        return held.at[pl.ds(index * items + start, size)]

    def halves(step):
        return range(1 if step == half - 1 else 2)

    def half_start(way, part):
        return (way + part) % 2 * (items // 2)

    def ring_owner(way, step):
        shift = n_rows - step if way == 0 else step
        return ring_index(lax.rem(place + shift, n_rows), n_rows)

    def ring_send_half(way, step, part):
        start, size = half_start(way, part), items // 2
        target = block_of(ring_owner(way, step), start, size)
        return remote(
            table_ref.at[pl.ds(start, size)] if step == 0 else target, target,
            ring_send.at[way, 2 * step + part], ring_recv.at[way, 2 * step + part],
            {"rows": right if way == 0 else left},
        )

    outs = []

    def keep(index, start, size):
        copy = pltpu.make_async_copy(
            block_of(index, start, size),
            gathered_ref.at[pl.ds(index * items + start, size)],
            out_sem.at[len(outs)],
        )
        copy.start()
        outs.append(copy)

    def add_gram(index, start, size):
        block = held[pl.ds(index * items + start, size), :]
        gram_ref[...] += dot(block, block, ((0,), (0,)))

    mine_users = pl.ds(me_row * users_dev, users_dev)
    first = [
        remote(users_ref, users.at[me_dim, mine_users], first_send.at[k], first_recv.at[k], {"rows": row_peer(k)})
        for k in range(1, n_rows)
    ]
    ring = {}
    for part in halves(0):
        for way in (0, 1):
            ring[way, 0, part] = ring_send_half(way, 0, part)
    table_far = [
        remote(table_ref, tables.at[me_dim], table_send.at[k], table_recv.at[k], {"dim": dim_peer(k)})
        for k in range(1, levels)
    ]
    table_near = [remote(table_ref, tables.at[me_dim], table_send.at[0], table_recv.at[0], {"dim": partner})]
    held[pl.ds(me_row * items, items), :] = table_ref[...]
    tables[me_dim] = table_ref[...]
    users[me_dim, mine_users, :] = users_ref[...]
    gram_ref[...] = jnp.zeros_like(gram_ref)
    keep(me_row, 0, items)
    add_gram(me_row, 0, items)

    for copy in first:
        copy.wait_recv()
    users_far = [
        remote(users.at[me_dim], users.at[me_dim], users_send.at[k], users_recv.at[k], {"dim": dim_peer(k)})
        for k in range(1, levels)
    ]
    users_near = [remote(users.at[me_dim], users.at[me_dim], users_send.at[0], users_recv.at[0], {"dim": partner})]
    sums = []

    def relay():
        for k in range(1, levels):
            source = dim_source(k)
            table_far[k - 1].wait_recv()
            table_near.append(remote(
                tables.at[source], tables.at[source], table_send.at[levels + k], table_recv.at[levels + k], {"dim": partner},
            ))
            users_far[k - 1].wait_recv()
            users_near.append(remote(
                users.at[source], users.at[source], users_send.at[levels + k], users_recv.at[levels + k], {"dim": partner},
            ))

    def score():
        for copy in table_near + users_near:
            copy.wait_recv()
        total = n_rows * users_dev
        chunk = min(256, total)
        pieces_of_table = table_ref[...]
        for start in range(0, total, chunk):
            scores = dot(users[0, start:start + chunk, :], tables[0], ((1,), (1,)))
            for d in range(1, n_dim):
                scores = scores + dot(users[d, start:start + chunk, :], tables[d], ((1,), (1,)))
            part = sum(dot(piece, pieces_of_table, ((1,), (0,))) for piece in split3(scores))
            staged[start:start + chunk, :] = part
        for k in range(1, n_rows):
            sums.append(remote(
                staged.at[pl.ds(row_peer(k) * users_dev, users_dev)], arrived.at[k],
                sum_send.at[k], sum_recv.at[k], {"rows": row_peer(k)},
            ))

    for step in range(half):
        for part in halves(step):
            for way in (0, 1):
                ring[way, step, part].wait_recv()
                if step < half - 1 and part in halves(step + 1):
                    ring[way, step + 1, part] = ring_send_half(way, step + 1, part)
            for way in (0, 1):
                found = (ring_owner(way, step + 1), half_start(way, part), items // 2)
                keep(*found)
                add_gram(*found)
        if step == 0:
            relay()
        if step == 1:
            score()

    times = staged[mine_users, :]
    for k in range(1, n_rows):
        sums[k - 1].wait_recv()
        times = times + arrived[k]
    times_ref[...] = times
    for copy in first + table_far + table_near + users_far + users_near + sums + list(ring.values()):
        copy.wait_send()
    for copy in outs:
        copy.wait()


def exchange(item_table, user_rows, n_rows, n_dim):
    items, width = item_table.shape
    users_dev = user_rows.shape[0]
    vmem = pl.BlockSpec(memory_space=pltpu.VMEM)
    dma = pltpu.SemaphoreType.DMA
    half = n_rows // 2
    return pl.pallas_call(
        functools.partial(exchange_kernel, n_rows, n_dim),
        out_shape=[
            jax.ShapeDtypeStruct((n_rows * items, width), BF16),
            jax.ShapeDtypeStruct((width, width), F32),
            jax.ShapeDtypeStruct((users_dev, width), F32),
        ],
        in_specs=[vmem] * 2,
        out_specs=[pl.BlockSpec(memory_space=pl.ANY), vmem, vmem],
        scratch_shapes=[
            pltpu.VMEM((n_rows * items, width), BF16),
            pltpu.VMEM((n_dim, items, width), BF16),
            pltpu.VMEM((n_dim, n_rows * users_dev, width), BF16),
            pltpu.VMEM((n_rows * users_dev, width), F32),
            pltpu.VMEM((n_rows, users_dev, width), F32),
            dma((2, 2 * half)),
            dma((2, 2 * half)),
            dma((2 * n_rows,)),
            dma((n_rows,)),
            dma((n_rows,)),
            dma((n_dim,)),
            dma((n_dim,)),
            dma((n_dim,)),
            dma((n_dim,)),
            dma((n_rows,)),
            dma((n_rows,)),
        ],
        compiler_params=pltpu.CompilerParams(
            collective_id=0, has_side_effects=True, vmem_limit_bytes=56 * 1024 * 1024
        ),
        name="exchange",
    )(item_table, user_rows)


def on_device(user_rows, item_table, observed_items, counts, item_row):
    width = user_rows.shape[1]
    users_dev, list_len = observed_items.shape
    weight_unobs = 32.0 / item_row.shape[0]
    vmem = pl.BlockSpec(memory_space=pltpu.VMEM)

    shard_rows, diag_gram, gram_times = exchange(
        item_table, user_rows, lax.axis_size("rows"), lax.axis_size("dim")
    )

    slots = observed_items.reshape(-1, 1)
    lines = item_row.reshape(-1, 128).astype(F32)
    line_of = lax.broadcasted_iota(jnp.int32, (1, lines.shape[0]), 1) == slots // 128
    chosen = exact_dot(line_of.astype(F32), lines, ((1,), (0,)))
    lane_of = lax.broadcasted_iota(jnp.int32, (1, 128), 1) == slots % 128
    table_rows = jnp.sum(jnp.where(lane_of, chosen, 0.0), axis=1).astype(jnp.int32)
    table_rows = table_rows.reshape(observed_items.shape)
    live = lax.broadcasted_iota(jnp.int32, (users_dev, list_len), 1) < counts[:, None]
    picked = shard_rows[table_rows]
    fetched = jnp.where(live[..., None], picked, jnp.zeros_like(picked))
    partial_value = jnp.einsum("ub,ujb->uj", user_rows, fetched, preferred_element_type=F32)
    n_dim = lax.axis_size("dim")
    predicted = partial_value
    for k in range(1, n_dim):
        pairs = [(d, (d + k) % n_dim) for d in range(n_dim)]
        predicted = predicted + lax.ppermute(partial_value, "dim", pairs)

    inverse = pl.pallas_call(
        functools.partial(inverse_kernel, weight_unobs),
        out_shape=jax.ShapeDtypeStruct((width, width), F32),
        in_specs=[vmem],
        out_specs=vmem,
        scratch_shapes=[pltpu.VMEM((width, width), F32)],
        cost_estimate=pl.CostEstimate(flops=20_000_000_000, bytes_accessed=524288, transcendentals=0),
        name="inverse",
    )(diag_gram)
    return pl.pallas_call(
        functools.partial(solve_kernel, weight_unobs),
        out_shape=jax.ShapeDtypeStruct((users_dev, width), F32),
        in_specs=[vmem] * 6,
        out_specs=vmem,
        scratch_shapes=[
            pltpu.VMEM((8, 128), F32),
            pltpu.VMEM((users_dev * list_len, list_len), F32),
            pltpu.VMEM((list_len, list_len + 8, users_dev), F32),
        ],
        compiler_params=pltpu.CompilerParams(vmem_limit_bytes=48 * 1024 * 1024),
        name="solve",
    )(
        fetched.reshape(users_dev * list_len, width), live.astype(F32), predicted, inverse,
        gram_times, user_rows,
    )


def solution(mesh):
    in_specs = (P("rows", "dim"), P("rows", "dim"), P("rows", None), P("rows"), P())
    out_specs = P("rows", "dim")
    return jax.shard_map(
        on_device, mesh=mesh, in_specs=in_specs, out_specs=out_specs, check_vma=False
    )
```

```python
import functools

import jax
import jax.numpy as jnp
from jax import lax
from jax.experimental import pallas as pl
from jax.experimental.pallas import tpu as pltpu
from jax.sharding import PartitionSpec as P

F32 = jnp.float32
BF16 = jnp.bfloat16
HIGHEST = lax.Precision.HIGHEST
PANEL = 32
GROUP = 8


def split3(x):
    high = x.astype(BF16)
    rest = x - high.astype(F32)
    middle = rest.astype(BF16)
    low = (rest - middle.astype(F32)).astype(BF16)
    return high, middle, low


def dot(a, b, dims):
    return lax.dot_general(a, b, (dims, ((), ())), preferred_element_type=F32)


def exact_dot(a, b, dims):
    return lax.dot_general(
        a, b, (dims, ((), ())), precision=HIGHEST, preferred_element_type=F32
    )


def inverse_kernel(weight, gram_ref, out_ref, work):
    width = gram_ref.shape[0]
    rows = lax.broadcasted_iota(jnp.int32, (width, width), 0)
    columns = lax.broadcasted_iota(jnp.int32, (width, width), 1)
    work[...] = weight * gram_ref[...] + jnp.where(rows == columns, 1.0, 0.0)
    panel_rows = lax.broadcasted_iota(jnp.int32, (PANEL, 1), 0)
    panel_columns = lax.broadcasted_iota(jnp.int32, (PANEL, width), 1)
    for panel in range(width // PANEL):
        first = panel * PANEL
        mine = (panel_columns >= first) & (panel_columns < first + PANEL)
        before = work[first:first + PANEL, :]
        after = before
        for group in range(0, PANEL, GROUP):
            spread = [
                jnp.broadcast_to(after[:, c:c + 1], (PANEL, 128))
                for c in range(first + group, first + group + GROUP)
            ]
            for step in range(group, group + GROUP):
                column = spread[step - group]
                inverse = 1.0 / column[step:step + 1, :]
                for later in range(step - group + 1, GROUP):
                    other = spread[later]
                    scaled = other[step:step + 1, :] * inverse
                    spread[later] = jnp.where(panel_rows == step, scaled, other - column * scaled)
                wide = jnp.concatenate([column] * (width // 128), axis=1)
                wide_inverse = jnp.concatenate([inverse] * (width // 128), axis=1)
                unit = jnp.where(panel_rows == step, 1.0, 0.0)
                after = jnp.where(panel_columns == first + step, unit, after)
                scaled = after[step:step + 1, :] * wide_inverse
                after = jnp.where(panel_rows == step, scaled, after - wide * scaled)
        after = jnp.where(mine, -after, after)
        sign = jnp.where(panel_columns == first + lax.broadcasted_iota(jnp.int32, (PANEL, width), 0), -1.0, 0.0)
        before = jnp.where(mine, sign, before)
        b1, b2, b3 = split3(before)
        a1, a2, a3 = split3(after)
        left = jnp.concatenate([b1, b1, b2, b1, b2, b3], axis=0)
        right = jnp.concatenate([a1, a2, a1, a3, a2, a1], axis=0)
        change = dot(left, right, ((0,), (0,)))
        outside = ((rows < first) | (rows >= first + PANEL)) & (
            (columns < first) | (columns >= first + PANEL)
        )
        work[...] = jnp.where(outside, work[...], 0.0) - change
    out_ref[...] = -work[...]


def own_slots(users, list_len):
    row = lax.broadcasted_iota(jnp.int32, (users, users * list_len), 0)
    column = lax.broadcasted_iota(jnp.int32, (users, users * list_len), 1)
    return (column >= row * list_len) & (column < (row + 1) * list_len)


def fold_lanes(x, list_len):
    lanes = 128
    total = x[:, :lanes]
    for part in range(1, x.shape[1] // lanes):
        total = total + x[:, part * lanes:(part + 1) * lanes]
    result = total[:, :list_len]
    for part in range(1, lanes // list_len):
        result = result + total[:, part * list_len:(part + 1) * list_len]
    return result


def spread_lanes(x, users):
    lanes = 128
    tile = jnp.concatenate([x] * (lanes // x.shape[1]), axis=1)
    return jnp.concatenate([tile] * (users * x.shape[1] // lanes), axis=1)


def solve_kernel(
    weight, rows_ref, live_ref, predicted_ref, inverse_ref, times_ref, own_ref, out_ref,
    scaled, folded, system,
):
    users, list_len = live_ref.shape
    own = own_ref[...].astype(F32)
    h = rows_ref[...]
    mask = own_slots(users, list_len)
    residual = live_ref[...] * (predicted_ref[...] - 1.0)
    spread = jnp.where(mask, spread_lanes(residual, users), 0.0)
    gradient = weight * times_ref[...] + own
    for piece in split3(spread):
        gradient = gradient + dot(piece, h, ((1,), (0,)))
    inverse = inverse_ref[...]
    scaled_grad = exact_dot(gradient, inverse, ((1,), (0,)))
    projected = jnp.zeros((users, users * list_len), F32)
    for piece in split3(scaled_grad):
        projected = projected + dot(piece, h, ((1,), (1,)))
    projected = fold_lanes(jnp.where(mask, projected, 0.0), list_len).T

    inverse_pieces = split3(inverse)
    group = 8 * list_len
    block_row = lax.broadcasted_iota(jnp.int32, (group, group), 0) // list_len
    block_column = lax.broadcasted_iota(jnp.int32, (group, group), 1) // list_len
    for start in range(0, users * list_len, group):
        here = rows_ref[start:start + group, :]
        x = sum(dot(here, piece, ((1,), (0,))) for piece in inverse_pieces)
        inner = sum(dot(piece, here, ((1,), (1,))) for piece in split3(x))
        inner = jnp.where(block_row == block_column, inner, 0.0)
        folded[start:start + group, :] = fold_lanes(inner, list_len)
    slot = lax.broadcasted_iota(jnp.int32, (list_len, users), 0)
    head = lax.broadcasted_iota(jnp.int32, (8, users), 0)
    for i in range(list_len):
        block = folded[pl.ds(i, users, stride=list_len), :].T
        system[i, :list_len, :] = block + jnp.where(slot == i, 1.0, 0.0)
        system[i, list_len:, :] = jnp.where(head == 0, projected[i:i + 1, :], 0.0)
    for k in range(list_len):
        first = k // 8 * 8
        pivot_row = system[k, first:, :]
        pivot_row = pivot_row * (1.0 / system[k, k:k + 1, :])
        for i in range(list_len):
            if i != k:
                system[i, first:, :] = system[i, first:, :] - system[i, k:k + 1, :] * pivot_row
    weights = jnp.concatenate(
        [system[i, list_len:list_len + 1, :] / system[i, i:i + 1, :] for i in range(list_len)], axis=0
    ).T
    spread = jnp.where(mask, spread_lanes(weights, users), 0.0)
    for piece in split3(spread):
        gradient = gradient - dot(piece, h, ((1,), (0,)))
    out_ref[...] = own - exact_dot(gradient, inverse, ((1,), (0,)))


MESH = pl.DeviceIdType.MESH


def ring_place(index, n):
    odd = lax.rem(index, 2)
    return (1 - odd) * lax.div(index, 2) + odd * (n // 2 + lax.div(n - 1 - index, 2))


def ring_index(place, n):
    high = lax.div(place, n // 2)
    return (1 - high) * 2 * place + high * (n - 1 - 2 * (place - n // 2))


def exchange_kernel(
    n_rows, n_dim, table_ref, users_ref, gathered_ref, gram_ref, times_ref,
    held, tables, users, staged, arrived,
    ring_send, ring_recv, out_sem, first_send, first_recv, table_send, table_recv,
    users_send, users_recv, sum_send, sum_recv,
):
    me_row = lax.axis_index("rows")
    me_dim = lax.axis_index("dim")
    items, width = table_ref.shape
    users_dev = users_ref.shape[0]
    half = n_rows // 2
    levels = n_dim // 2
    core = lax.rem(me_dim, 2)
    partner = me_dim + 1 - 2 * core
    place = ring_place(me_row, n_rows)
    right = ring_index(lax.rem(place + 1, n_rows), n_rows)
    left = ring_index(lax.rem(place + n_rows - 1, n_rows), n_rows)

    def row_peer(k):
        return lax.rem(me_row + k, n_rows)

    def dim_peer(k):
        return lax.rem(me_dim + 2 * k, n_dim)

    def dim_source(k):
        return lax.rem(me_dim + n_dim - 2 * k, n_dim)

    barrier = pltpu.get_barrier_semaphore()
    for k in range(1, n_rows):
        pl.semaphore_signal(barrier, inc=1, device_id={"rows": row_peer(k)}, device_id_type=MESH)
    for k in range(1, levels):
        pl.semaphore_signal(barrier, inc=1, device_id={"dim": dim_peer(k)}, device_id_type=MESH)
    pl.semaphore_signal(barrier, inc=1, device_id={"dim": partner}, device_id_type=MESH)
    pl.semaphore_wait(barrier, n_rows - 1 + levels)

    def remote(src, dst, send, recv, device):
        copy = pltpu.make_async_remote_copy(
            src_ref=src, dst_ref=dst, send_sem=send, recv_sem=recv,
            device_id=device, device_id_type=MESH,
        )
        copy.start()
        return copy

    def block_of(index, start, size):
        return held.at[pl.ds(index * items + start, size)]

    def halves(step):
        return range(1 if step == half - 1 else 2)

    def half_start(way, part):
        return (way + part) % 2 * (items // 2)

    def ring_owner(way, step):
        shift = n_rows - step if way == 0 else step
        return ring_index(lax.rem(place + shift, n_rows), n_rows)

    def ring_send_half(way, step, part):
        start, size = half_start(way, part), items // 2
        target = block_of(ring_owner(way, step), start, size)
        return remote(
            table_ref.at[pl.ds(start, size)] if step == 0 else target, target,
            ring_send.at[way, 2 * step + part], ring_recv.at[way, 2 * step + part],
            {"rows": right if way == 0 else left},
        )

    outs = []

    def keep(index, start, size):
        copy = pltpu.make_async_copy(
            block_of(index, start, size),
            gathered_ref.at[pl.ds(index * items + start, size)],
            out_sem.at[len(outs)],
        )
        copy.start()
        outs.append(copy)

    def add_gram(index, start, size):
        block = held[pl.ds(index * items + start, size), :]
        gram_ref[...] += dot(block, block, ((0,), (0,)))

    mine_users = pl.ds(me_row * users_dev, users_dev)
    ring = {}
    for part in halves(0):
        for way in (0, 1):
            ring[way, 0, part] = ring_send_half(way, 0, part)
    first = [
        remote(users_ref, users.at[me_dim, mine_users], first_send.at[k], first_recv.at[k], {"rows": row_peer(k)})
        for k in range(1, n_rows)
    ]
    table_far = [
        remote(table_ref, tables.at[me_dim], table_send.at[k], table_recv.at[k], {"dim": dim_peer(k)})
        for k in range(1, levels)
    ]
    table_near = [remote(table_ref, tables.at[me_dim], table_send.at[0], table_recv.at[0], {"dim": partner})]
    held[pl.ds(me_row * items, items), :] = table_ref[...]
    tables[me_dim] = table_ref[...]
    users[me_dim, mine_users, :] = users_ref[...]
    gram_ref[...] = jnp.zeros_like(gram_ref)
    keep(me_row, 0, items)
    add_gram(me_row, 0, items)

    users_far, users_near = [], []

    def share_users():
        for copy in first:
            copy.wait_recv()
        for k in range(1, levels):
            users_far.append(remote(
                users.at[me_dim], users.at[me_dim], users_send.at[k], users_recv.at[k], {"dim": dim_peer(k)},
            ))
        users_near.append(remote(
            users.at[me_dim], users.at[me_dim], users_send.at[0], users_recv.at[0], {"dim": partner},
        ))

    sums = []

    def relay():
        for k in range(1, levels):
            source = dim_source(k)
            table_far[k - 1].wait_recv()
            table_near.append(remote(
                tables.at[source], tables.at[source], table_send.at[levels + k], table_recv.at[levels + k], {"dim": partner},
            ))
            users_far[k - 1].wait_recv()
            users_near.append(remote(
                users.at[source], users.at[source], users_send.at[levels + k], users_recv.at[levels + k], {"dim": partner},
            ))

    def score():
        for copy in table_near + users_near:
            copy.wait_recv()
        total = n_rows * users_dev
        chunk = min(256, total)
        pieces_of_table = table_ref[...]
        for start in range(0, total, chunk):
            scores = dot(users[0, start:start + chunk, :], tables[0], ((1,), (1,)))
            for d in range(1, n_dim):
                scores = scores + dot(users[d, start:start + chunk, :], tables[d], ((1,), (1,)))
            part = sum(dot(piece, pieces_of_table, ((1,), (0,))) for piece in split3(scores))
            staged[start:start + chunk, :] = part
        for k in range(1, n_rows):
            sums.append(remote(
                staged.at[pl.ds(row_peer(k) * users_dev, users_dev)], arrived.at[k],
                sum_send.at[k], sum_recv.at[k], {"rows": row_peer(k)},
            ))

    for step in range(half):
        for part in halves(step):
            for way in (0, 1):
                ring[way, step, part].wait_recv()
                if step < half - 1 and part in halves(step + 1):
                    ring[way, step + 1, part] = ring_send_half(way, step + 1, part)
            for way in (0, 1):
                found = (ring_owner(way, step + 1), half_start(way, part), items // 2)
                keep(*found)
                add_gram(*found)
        if step == 0:
            share_users()
        if step == 1:
            relay()
        if step == 2:
            score()

    times = staged[mine_users, :]
    for k in range(1, n_rows):
        sums[k - 1].wait_recv()
        times = times + arrived[k]
    times_ref[...] = times
    for copy in first + table_far + table_near + users_far + users_near + sums + list(ring.values()):
        copy.wait_send()
    for copy in outs:
        copy.wait()


def exchange(item_table, user_rows, n_rows, n_dim):
    items, width = item_table.shape
    users_dev = user_rows.shape[0]
    vmem = pl.BlockSpec(memory_space=pltpu.VMEM)
    dma = pltpu.SemaphoreType.DMA
    half = n_rows // 2
    return pl.pallas_call(
        functools.partial(exchange_kernel, n_rows, n_dim),
        out_shape=[
            jax.ShapeDtypeStruct((n_rows * items, width), BF16),
            jax.ShapeDtypeStruct((width, width), F32),
            jax.ShapeDtypeStruct((users_dev, width), F32),
        ],
        in_specs=[vmem] * 2,
        out_specs=[pl.BlockSpec(memory_space=pl.ANY), vmem, vmem],
        scratch_shapes=[
            pltpu.VMEM((n_rows * items, width), BF16),
            pltpu.VMEM((n_dim, items, width), BF16),
            pltpu.VMEM((n_dim, n_rows * users_dev, width), BF16),
            pltpu.VMEM((n_rows * users_dev, width), F32),
            pltpu.VMEM((n_rows, users_dev, width), F32),
            dma((2, 2 * half)),
            dma((2, 2 * half)),
            dma((2 * n_rows,)),
            dma((n_rows,)),
            dma((n_rows,)),
            dma((n_dim,)),
            dma((n_dim,)),
            dma((n_dim,)),
            dma((n_dim,)),
            dma((n_rows,)),
            dma((n_rows,)),
        ],
        compiler_params=pltpu.CompilerParams(
            collective_id=0, has_side_effects=True, vmem_limit_bytes=56 * 1024 * 1024
        ),
        name="exchange",
    )(item_table, user_rows)


def on_device(user_rows, item_table, observed_items, counts, item_row):
    width = user_rows.shape[1]
    users_dev, list_len = observed_items.shape
    weight_unobs = 32.0 / item_row.shape[0]
    vmem = pl.BlockSpec(memory_space=pltpu.VMEM)

    shard_rows, diag_gram, gram_times = exchange(
        item_table, user_rows, lax.axis_size("rows"), lax.axis_size("dim")
    )

    slots = observed_items.reshape(-1, 1)
    lines = item_row.reshape(-1, 128).astype(F32)
    line_of = lax.broadcasted_iota(jnp.int32, (1, lines.shape[0]), 1) == slots // 128
    chosen = exact_dot(line_of.astype(F32), lines, ((1,), (0,)))
    lane_of = lax.broadcasted_iota(jnp.int32, (1, 128), 1) == slots % 128
    table_rows = jnp.sum(jnp.where(lane_of, chosen, 0.0), axis=1).astype(jnp.int32)
    table_rows = table_rows.reshape(observed_items.shape)
    live = lax.broadcasted_iota(jnp.int32, (users_dev, list_len), 1) < counts[:, None]
    picked = shard_rows[table_rows]
    fetched = jnp.where(live[..., None], picked, jnp.zeros_like(picked))
    partial_value = jnp.einsum("ub,ujb->uj", user_rows, fetched, preferred_element_type=F32)
    n_dim = lax.axis_size("dim")
    predicted = partial_value
    for k in range(1, n_dim):
        pairs = [(d, (d + k) % n_dim) for d in range(n_dim)]
        predicted = predicted + lax.ppermute(partial_value, "dim", pairs)

    inverse = pl.pallas_call(
        functools.partial(inverse_kernel, weight_unobs),
        out_shape=jax.ShapeDtypeStruct((width, width), F32),
        in_specs=[vmem],
        out_specs=vmem,
        scratch_shapes=[pltpu.VMEM((width, width), F32)],
        cost_estimate=pl.CostEstimate(flops=20_000_000_000, bytes_accessed=524288, transcendentals=0),
        name="inverse",
    )(diag_gram)
    return pl.pallas_call(
        functools.partial(solve_kernel, weight_unobs),
        out_shape=jax.ShapeDtypeStruct((users_dev, width), F32),
        in_specs=[vmem] * 6,
        out_specs=vmem,
        scratch_shapes=[
            pltpu.VMEM((8, 128), F32),
            pltpu.VMEM((users_dev * list_len, list_len), F32),
            pltpu.VMEM((list_len, list_len + 8, users_dev), F32),
        ],
        compiler_params=pltpu.CompilerParams(vmem_limit_bytes=48 * 1024 * 1024),
        name="solve",
    )(
        fetched.reshape(users_dev * list_len, width), live.astype(F32), predicted, inverse,
        gram_times, user_rows,
    )


def solution(mesh):
    in_specs = (P("rows", "dim"), P("rows", "dim"), P("rows", None), P("rows"), P())
    out_specs = P("rows", "dim")
    return jax.shard_map(
        on_device, mesh=mesh, in_specs=in_specs, out_specs=out_specs, check_vma=False
    )
```
